32 devices in a mesh: groups: 2 (over y), rowt: 4 (over z), colt: 2 (over x), site: 2 (over core).
Axes of the slice: x: 2, y: 2, z: 4, core: 2. Of those that a mesh axis runs over, the one named last changes fastest.
Arguments:
- seed_green: bfloat16 [8, 2, 768, 768], P(('groups', 'rowt'), 'colt', None, 'site'), parts along dimension 0, may hold values from -6 to 6
- field_spins: int32 [4, 8, 768], P(None, ('groups', 'rowt')), parts along dimension 1, may hold values from 0 to 1
- hop_matrix: float32 [768, 768], replicated, may hold values from -0.21875 to 0.21875
- vertex: bfloat16 [768, 768], replicated, may hold values from -0.21875 to 0.21875
Outputs:
- measured: bfloat16 [8, 2, 768, 768], P(('groups', 'rowt'), 'colt', None, 'site'), parts along dimension 0
The draws below stay inside these ranges and needn't reach their ends.
There are 2 independent parts, one for each index of `groups`. The reference program is written for one: setup_inputs(seed, part) draws one part's arguments, and reference() takes and returns one part's arrays. A program takes and returns all parts, laid end to end along the dimension named above; an argument that names none is the same for every part. Nothing has to cross between parts.
All inputs are finite; a program needn't handle non-finite values.
Results may differ from the reference program's by a relative error of at most 0.0051.
Values may be sent and summed in bfloat16 or wider, within the bound.
A program may use at most 64 MiB of HBM per device.

```python
import jax
import jax.numpy as jnp
from jax import lax

N = 768
WRAPS = 4
TR = 4
TC = 2


def set_ends(result, rng, smallest, top_value):
    shape = result.shape
    spot = [jax.random.randint(jax.random.fold_in(rng, axis), (), 0, shape[axis]) for axis in range(len(shape))]
    result = result.at[tuple(spot)].set(smallest)
    longest = shape.index(max(shape))
    spot[longest] = (spot[longest] + 1) % shape[longest]
    return result.at[tuple(spot)].set(top_value)


def block_scale(own_key, dims, cuts, least, largest):
    def one(position, shards_of):
        steps = jax.random.uniform(jax.random.fold_in(jax.random.fold_in(own_key, 6), position), (shards_of,), jnp.float32, least / len(cuts), largest / len(cuts))
        return jnp.repeat(jnp.exp(steps), dims[position] // shards_of).reshape((-1,) + (1,) * (len(dims) - position - 1))

    loudness = one(*cuts[0])
    for cut in cuts[1:]:
        loudness = loudness * one(*cut)
    return loudness


def normal_values(own_key, extent, scale, bound, cuts=(), held_as=jnp.bfloat16):
    factor_of = block_scale(own_key, extent, cuts, -0.22, 0.18) if cuts else 1.0
    entries = jax.random.normal(own_key, extent, jnp.float32) * scale * factor_of
    return jnp.minimum(jnp.maximum(entries, -bound), bound).astype(held_as)


def setup_inputs(seed: int = 0, part: int = 0) -> dict:
    arg_keys = jax.random.split(jax.random.key(seed), 5)
    part_keys = jax.random.split(jax.random.fold_in(arg_keys[4], part), 5)
    seed_green = normal_values(part_keys[0], (TR, TC, N, N), 1.0, 6.0, ((0, 4), (1, 2), (3, 2)))
    field_spins = set_ends(jax.random.randint(part_keys[1], (WRAPS, TR, N), 0, 2), jax.random.fold_in(part_keys[1], 1), 0, 1).astype(jnp.int32)
    hop_matrix = normal_values(arg_keys[2], (N, N), N ** -0.5, 0.21875, (), jnp.float32)
    vertex = normal_values(arg_keys[3], (N, N), N ** -0.5, 0.21875)
    return {"seed_green": seed_green, "field_spins": field_spins, "hop_matrix": hop_matrix, "vertex": vertex}


coupling = 0.45
keep_share = 0.8
hop_share = 0.3


def reference(seed_green, field_spins, hop_matrix, vertex):
    row_count = seed_green.shape[0]
    col_count = seed_green.shape[1]
    weights = jnp.exp(coupling * (2.0 * field_spins.astype(jnp.float32) - 1.0))
    vertex_wide = vertex.astype(jnp.float32)

    def one_row(row_index):
        current = lax.dynamic_index_in_dim(seed_green, row_index, 0, keepdims=False).astype(jnp.float32)
        measured = jnp.zeros_like(current)
        for wrap_step in range(WRAPS):
            target = (row_index + wrap_step + 1) % row_count
            weights_row = lax.dynamic_index_in_dim(weights[wrap_step], target, 0, keepdims=False)
            sign_value = jnp.where(target == 0, -1.0, 1.0).astype(jnp.float32)
            hopped = jnp.einsum("ab,cbd->cad", hop_matrix, current, precision=lax.Precision.HIGHEST)
            image = keep_share * current + hop_share * hopped
            current = (sign_value * weights_row)[None, :, None] * image
            rounded = current.astype(jnp.bfloat16)
            partner = jnp.roll(rounded, col_count // 2, axis=0)
            pair_product = (rounded.astype(jnp.float32) * jnp.swapaxes(partner, 1, 2).astype(jnp.float32)).astype(jnp.bfloat16)
            measured = measured + jnp.einsum("ab,cbd->cad", vertex_wide, pair_product.astype(jnp.float32))
        return (measured / WRAPS).astype(jnp.bfloat16)

    return lax.map(one_row, jnp.arange(row_count, dtype=jnp.int32))
```

```python
import functools

import jax
import jax.numpy as jnp
from jax import lax
from jax.experimental import pallas as pl
from jax.experimental.pallas import tpu as pltpu
from jax.sharding import PartitionSpec as P

coupling = 0.45
keep_share = 0.8
hop_share = 0.3
MESH = pl.DeviceIdType.MESH
F32 = jnp.float32
BF16 = jnp.bfloat16


def split(x):
    high = x.astype(BF16)
    return high, (x - high.astype(F32)).astype(BF16)


def nn(a, b):
    return lax.dot_general(a, b, (((1,), (0,)), ((), ())), preferred_element_type=F32)


def nt(a, b):
    return lax.dot_general(a, b, (((1,), (1,)), ((), ())), preferred_element_type=F32)


def chunk_list(columns):
    chunks, start = [], 0
    while start < columns:
        width = min(256, columns - start)
        chunks.append((start, width))
        start += width
    return chunks


def kernel(
    rows_n, cols_n,
    seed, spins, hop, vertex, out,
    own, hop_v, vertex_v, spin_v, theirs, a_hi, a_lo, x_hi, x_lo, y_hi, y_lo, cross, t_hi, t_lo,
    local_sem, seed_send, seed_recv, spin_send, spin_recv, cross_send, cross_recv,
):
    order, columns = own.shape
    wraps = spins.shape[0]
    row = lax.axis_index("rowt")
    col = lax.axis_index("colt")
    site = lax.axis_index("site")
    other_site = 1 - site
    other_col = lax.rem(col + cols_n // 2, cols_n)
    chunks = chunk_list(columns)

    local = [
        pltpu.make_async_copy(seed.at[0, 0], own, local_sem.at[0]),
        pltpu.make_async_copy(hop, hop_v, local_sem.at[1]),
        pltpu.make_async_copy(vertex, vertex_v, local_sem.at[2]),
    ]
    for copy in local:
        copy.start()

    distances = sorted({(w + 1) % rows_n for w in range(wraps)} - {0})
    peers = sorted(set(distances) | {(-d) % rows_n for d in distances})
    barrier = pltpu.get_barrier_semaphore()
    for peer in peers:
        pl.semaphore_signal(
            barrier, inc=1, device_id={"rowt": lax.rem(row + peer, rows_n)}, device_id_type=MESH
        )
    pl.semaphore_signal(barrier, inc=1, device_id={"colt": other_col}, device_id_type=MESH)
    pl.semaphore_signal(barrier, inc=1, device_id={"site": other_site}, device_id_type=MESH)
    pl.semaphore_wait(barrier, len(peers) + 2)

    spin_copies = []
    for w in range(wraps):
        distance = (w + 1) % rows_n
        if distance == 0:
            copy = pltpu.make_async_copy(spins.at[w], spin_v.at[w], spin_recv.at[w])
        else:
            copy = pltpu.make_async_remote_copy(
                src_ref=spins.at[w],
                dst_ref=spin_v.at[w],
                send_sem=spin_send.at[w],
                recv_sem=spin_recv.at[w],
                device_id={"rowt": lax.rem(row + rows_n - distance, rows_n)},
                device_id_type=MESH,
            )
        copy.start()
        spin_copies.append(copy)
    seed_copies = []
    for c, (start, width) in enumerate(chunks):
        copy = pltpu.make_async_remote_copy(
            src_ref=seed.at[0, 0, :, pl.ds(start, width)],
            dst_ref=theirs.at[:, pl.ds(start, width)],
            send_sem=seed_send.at[c],
            recv_sem=seed_recv.at[c],
            device_id={"colt": other_col},
            device_id_type=MESH,
        )
        copy.start()
        seed_copies.append(copy)

    local[1].wait()
    step = 128
    for r in range(0, order, step):
        a = hop_share * hop_v[r:r + step, :]
        diagonal = lax.broadcasted_iota(jnp.int32, a.shape, 0) + r == lax.broadcasted_iota(
            jnp.int32, a.shape, 1
        )
        high, low = split(a + jnp.where(diagonal, F32(keep_share), F32(0)))
        a_hi[r:r + step, :] = high
        a_lo[r:r + step, :] = low

    local[0].wait()
    x0 = own[...].T

    def weight_row(w):
        sign = jnp.where(lax.rem(row + w + 1, rows_n) == 0, F32(-1), F32(1))
        return sign * jnp.exp(coupling * (2.0 * spin_v[w].astype(F32) - 1.0))

    tile = 256
    weights_col = []
    for w in range(wraps):
        for n in range(0, order, tile):
            high = a_hi[n:n + tile, :]
            low = a_lo[n:n + tile, :]
            if w == 0:
                product = nt(x0, high) + nt(x0, low)
            else:
                before = x_hi[w - 1]
                product = nt(before, high) + nt(before, low) + nt(x_lo[(w - 1) % 2], high)
            if n == 0:
                spin_copies[w].wait()
                weights = weight_row(w)
                weights_col.append(jnp.broadcast_to(weights, (128, order)).T)
            high, low = split(product * weights[:, n:n + tile])
            x_hi[w, :, n:n + tile] = high
            if w < wraps - 1:
                x_lo[w % 2, :, n:n + tile] = low

    row_of_other = pl.ds(pl.multiple_of(other_site * columns, columns), columns)
    row_of_own = pl.ds(pl.multiple_of(site * columns, columns), columns)
    cross_copies = []
    for c, (start, width) in enumerate(chunks):
        seed_copies[c].wait_recv()
        part = pl.ds(start, width)
        for w in range(wraps):
            if w == 0:
                before = theirs[:, start:start + width]
                product = nn(a_hi[...], before) + nn(a_lo[...], before)
            else:
                before = y_hi[w - 1, :, start:start + width]
                product = (
                    nn(a_hi[...], before) + nn(a_lo[...], before)
                    + nn(a_hi[...], y_lo[:, :width])
                )
            scale = jnp.concatenate([weights_col[w]] * (width // 128), axis=1)
            high, low = split(product * scale)
            y_hi[w, :, start:start + width] = high
            if w < wraps - 1:
                y_lo[:, :width] = low
            copy = pltpu.make_async_remote_copy(
                src_ref=y_hi.at[w, row_of_other, part],
                dst_ref=cross.at[w, :, part],
                send_sem=cross_send.at[c, w],
                recv_sem=cross_recv.at[c, w],
                device_id={"site": other_site},
                device_id_type=MESH,
            )
            copy.start()
            cross_copies.append(copy)

    def pair_sum(near, far):
        total = None
        for w in range(wraps):
            pair = (near(w).astype(F32) * far(w).astype(F32)).astype(BF16).astype(F32)
            total = pair if total is None else total + pair
        return split(total)

    own_lanes = pl.ds(pl.multiple_of(site * columns, columns), columns)
    other_lanes = pl.ds(pl.multiple_of(other_site * columns, columns), columns)
    high, low = pair_sum(lambda w: x_hi[w, :, own_lanes], lambda w: y_hi[w, row_of_own, :])
    t_hi[:, own_lanes] = high
    t_lo[:, own_lanes] = low
    for copy in cross_copies:
        copy.wait_recv()
    high, low = pair_sum(lambda w: x_hi[w, :, other_lanes], lambda w: cross[w])
    t_hi[:, other_lanes] = high
    t_lo[:, other_lanes] = low

    local[2].wait()
    for m in range(0, order, tile):
        v = vertex_v[m:m + tile, :]
        out[0, 0, m:m + tile, :] = ((nt(v, t_hi[...]) + nt(v, t_lo[...])) / wraps).astype(BF16)

    for copy in seed_copies + cross_copies:
        copy.wait_send()


def per_device(rows_n, cols_n, seed_green, field_spins, hop_matrix, vertex):
    wraps = field_spins.shape[0]
    order, columns = seed_green.shape[2:]
    n_chunks = len(chunk_list(columns))
    dma = pltpu.SemaphoreType.DMA
    any_space = pl.BlockSpec(memory_space=pl.ANY)
    return pl.pallas_call(
        functools.partial(kernel, rows_n, cols_n),
        out_shape=jax.ShapeDtypeStruct(seed_green.shape, BF16),
        in_specs=[any_space] * 4,
        out_specs=pl.BlockSpec(memory_space=pltpu.VMEM),
        scratch_shapes=[
            pltpu.VMEM((order, columns), BF16),
            pltpu.VMEM((order, order), F32),
            pltpu.VMEM((order, order), BF16),
            pltpu.VMEM((wraps, 1, order), jnp.int32),
            pltpu.VMEM((order, columns), BF16),
            pltpu.VMEM((order, order), BF16),
            pltpu.VMEM((order, order), BF16),
            pltpu.VMEM((wraps, columns, order), BF16),
            pltpu.VMEM((2, columns, order), BF16),
            pltpu.VMEM((wraps, order, columns), BF16),
            pltpu.VMEM((order, 256), BF16),
            pltpu.VMEM((wraps, columns, columns), BF16),
            pltpu.VMEM((columns, order), BF16),
            pltpu.VMEM((columns, order), BF16),
            dma((3,)),
            dma((n_chunks,)),
            dma((n_chunks,)),
            dma((wraps,)),
            dma((wraps,)),
            dma((n_chunks, wraps)),
            dma((n_chunks, wraps)),
        ],
        compiler_params=pltpu.CompilerParams(
            collective_id=0, has_side_effects=True, vmem_limit_bytes=62 * 1024 * 1024
        ),
    )(seed_green, field_spins, hop_matrix, vertex)


def solution(mesh):
    body = functools.partial(per_device, mesh.shape["rowt"], mesh.shape["colt"])
    return jax.shard_map(
        body,
        mesh=mesh,
        in_specs=(
            P(("groups", "rowt"), "colt", None, "site"),
            P(None, ("groups", "rowt"), None),
            P(),
            P(),
        ),
        out_specs=P(("groups", "rowt"), "colt", None, "site"),
        check_vma=False,
    )
```

```python
import functools

import jax
import jax.numpy as jnp
from jax import lax
from jax.experimental import pallas as pl
from jax.experimental.pallas import tpu as pltpu
from jax.sharding import PartitionSpec as P

coupling = 0.45
keep_share = 0.8
hop_share = 0.3
MESH = pl.DeviceIdType.MESH
F32 = jnp.float32
BF16 = jnp.bfloat16


def split(x):
    high = x.astype(BF16)
    return high, (x - high.astype(F32)).astype(BF16)


def nn(a, b):
    return lax.dot_general(a, b, (((1,), (0,)), ((), ())), preferred_element_type=F32)


def nt(a, b):
    return lax.dot_general(a, b, (((1,), (1,)), ((), ())), preferred_element_type=F32)


def kernel(
    rows_n, cols_n,
    seed, spins, hop, vertex, out,
    own, hop_v, vertex_v, spin_v, theirs, a_hi, a_lo, x_hi, x_lo, y_hi, y_lo, m_hi, m_lo, total_v,
    local_sem, seed_send, seed_recv, pass_send, pass_recv, spin_send, spin_recv, cross_send,
    cross_recv,
):
    order, columns = own.shape
    wraps = spins.shape[0]
    row = lax.axis_index("rowt")
    col = lax.axis_index("colt")
    site = lax.axis_index("site")
    other_site = 1 - site
    other_col = lax.rem(col + cols_n // 2, cols_n)
    lanes = 128
    chunks = columns // lanes
    own_lanes = pl.ds(pl.multiple_of(site * columns, lanes), columns)
    row_of_other = pl.ds(pl.multiple_of(other_site * columns, lanes), columns)
    row_of_own = pl.ds(pl.multiple_of(site * columns, lanes), columns)

    local = [
        pltpu.make_async_copy(seed.at[0, 0], own, local_sem.at[0]),
        pltpu.make_async_copy(hop, hop_v, local_sem.at[1]),
        pltpu.make_async_copy(vertex, vertex_v, local_sem.at[2]),
    ]
    for copy in local:
        copy.start()

    distances = sorted({(w + 1) % rows_n for w in range(wraps)} - {0})
    peers = sorted(set(distances) | {(-d) % rows_n for d in distances})
    barrier = pltpu.get_barrier_semaphore()
    for peer in peers:
        pl.semaphore_signal(
            barrier, inc=1, device_id={"rowt": lax.rem(row + peer, rows_n)}, device_id_type=MESH
        )
    pl.semaphore_signal(barrier, inc=1, device_id={"colt": other_col}, device_id_type=MESH)
    pl.semaphore_signal(barrier, inc=1, device_id={"site": other_site}, device_id_type=MESH)
    pl.semaphore_wait(barrier, len(peers) + 2)

    spin_copies = []
    for w in range(wraps):
        distance = (w + 1) % rows_n
        if distance == 0:
            copy = pltpu.make_async_copy(spins.at[w], spin_v.at[w], spin_recv.at[w])
        else:
            copy = pltpu.make_async_remote_copy(
                src_ref=spins.at[w],
                dst_ref=spin_v.at[w],
                send_sem=spin_send.at[w],
                recv_sem=spin_recv.at[w],
                device_id={"rowt": lax.rem(row + rows_n - distance, rows_n)},
                device_id_type=MESH,
            )
        copy.start()
        spin_copies.append(copy)
    seed_copies, pass_copies = [], []
    for c in range(chunks):
        spot = pl.ds(pl.multiple_of(site * columns + c * lanes, lanes), lanes)
        seed_copies.append(pltpu.make_async_remote_copy(
            src_ref=seed.at[0, 0, :, pl.ds(c * lanes, lanes)],
            dst_ref=theirs.at[:, spot],
            send_sem=seed_send.at[c],
            recv_sem=seed_recv.at[c],
            device_id={"colt": other_col},
            device_id_type=MESH,
        ))
        pass_copies.append(pltpu.make_async_remote_copy(
            src_ref=theirs.at[:, spot],
            dst_ref=theirs.at[:, spot],
            send_sem=pass_send.at[c],
            recv_sem=pass_recv.at[c],
            device_id={"site": other_site},
            device_id_type=MESH,
        ))
        seed_copies[c].start()

    def pass_on(c):
        seed_copies[c].wait_recv()
        pass_copies[c].start()

    local[1].wait()
    step = 128
    for r in range(0, order, step):
        a = hop_share * hop_v[r:r + step, :]
        diagonal = lax.broadcasted_iota(jnp.int32, a.shape, 0) + r == lax.broadcasted_iota(
            jnp.int32, a.shape, 1
        )
        high, low = split(a + jnp.where(diagonal, F32(keep_share), F32(0)))
        a_hi[r:r + step, :] = high
        a_lo[r:r + step, :] = low

    local[0].wait()
    x0 = own[...].T

    def weight_row(w):
        sign = jnp.where(lax.rem(row + w + 1, rows_n) == 0, F32(-1), F32(1))
        return sign * jnp.exp(coupling * (2.0 * spin_v[w].astype(F32) - 1.0))

    tile = 256
    cross_copies = []
    for w in range(wraps):
        products = []
        for n in range(0, order, tile):
            high = a_hi[n:n + tile, :]
            low = a_lo[n:n + tile, :]
            if w == 0:
                product = nt(x0, high) + nt(x0, low)
            else:
                before = x_hi[w - 1]
                product = nt(before, high) + nt(before, low) + nt(x_lo[(w - 1) % 2], high)
            if n == 0:
                spin_copies[w].wait()
                weights = weight_row(w)
            high, low = split(product * weights[:, n:n + tile])
            x_hi[w, :, n:n + tile] = high
            if w < wraps - 1:
                x_lo[w % 2, :, n:n + tile] = low
        if w == 0:
            product = a_hi[:, own_lanes].astype(F32) + a_lo[:, own_lanes].astype(F32)
        else:
            product = (
                nn(a_hi[...], y_hi[w - 1]) + nn(a_lo[...], y_hi[w - 1])
                + nn(a_hi[...], y_lo[w - 1])
            )
        column = jnp.broadcast_to(weights, (lanes, order)).T
        high, low = split(product * jnp.concatenate([column] * chunks, axis=1))
        for part, (value, held, whole) in enumerate(((high, y_hi, m_hi), (low, y_lo, m_lo))):
            held[w] = value
            copy = pltpu.make_async_remote_copy(
                src_ref=held.at[w, row_of_other],
                dst_ref=whole.at[w, :, own_lanes],
                send_sem=cross_send.at[part, w],
                recv_sem=cross_recv.at[part, w],
                device_id={"site": other_site},
                device_id_type=MESH,
            )
            copy.start()
            cross_copies.append(copy)
            whole[w, :, own_lanes] = held[w, row_of_own]
        if w == wraps - 2:
            pass_on(0)

    def both(c):
        return [s * columns + c * lanes for s in range(2)]

    def take(ref, index, c):
        return jnp.concatenate([ref[index + (slice(a, a + lanes),)] for a in both(c)], axis=1)

    def pair_sum(c):
        pass_copies[c].wait_recv()
        block = take(theirs, (slice(None),), c)
        total = None
        for w in range(wraps):
            far = (nn(m_hi[w], block) + nn(m_lo[w], block)).astype(BF16)
            near = take(x_hi, (w, slice(None)), c)
            pair = (near.astype(F32) * far.astype(F32)).astype(BF16).astype(F32)
            total = pair if total is None else total + pair
        return split(total)

    if wraps < 2:
        pass_on(0)
    if chunks > 2:
        pass_on(1)
    for copy in cross_copies:
        copy.wait_recv()
    sums = []
    for c in range(chunks - 1):
        if 1 < c + 1 < chunks - 1:
            pass_on(c + 1)
        sums.append(pair_sum(c))
    if chunks > 1:
        pass_on(chunks - 1)
    local[2].wait()
    high = jnp.concatenate([h for h, _ in sums], axis=1)
    low = jnp.concatenate([l for _, l in sums], axis=1)
    for m in range(0, order, tile):
        rows = slice(m, m + tile)
        v = jnp.concatenate([take(vertex_v, (rows,), c) for c in range(chunks - 1)], axis=1)
        total_v[rows] = nt(v, high) + nt(v, low)
    high, low = pair_sum(chunks - 1)
    for m in range(0, order, tile):
        rows = slice(m, m + tile)
        v = take(vertex_v, (rows,), chunks - 1)
        total = total_v[rows] + nt(v, high) + nt(v, low)
        out[0, 0, rows] = (total / wraps).astype(BF16)

    for copy in seed_copies + pass_copies + cross_copies:
        copy.wait_send()


def per_device(rows_n, cols_n, seed_green, field_spins, hop_matrix, vertex):
    wraps = field_spins.shape[0]
    order, columns = seed_green.shape[2:]
    n_chunks = columns // 128
    dma = pltpu.SemaphoreType.DMA
    any_space = pl.BlockSpec(memory_space=pl.ANY)
    return pl.pallas_call(
        functools.partial(kernel, rows_n, cols_n),
        out_shape=jax.ShapeDtypeStruct(seed_green.shape, BF16),
        in_specs=[any_space] * 4,
        out_specs=pl.BlockSpec(memory_space=pltpu.VMEM),
        scratch_shapes=[
            pltpu.VMEM((order, columns), BF16),
            pltpu.VMEM((order, order), F32),
            pltpu.VMEM((order, order), BF16),
            pltpu.VMEM((wraps, 1, order), jnp.int32),
            pltpu.VMEM((order, order), BF16),
            pltpu.VMEM((order, order), BF16),
            pltpu.VMEM((order, order), BF16),
            pltpu.VMEM((wraps, columns, order), BF16),
            pltpu.VMEM((2, columns, order), BF16),
            pltpu.VMEM((wraps, order, columns), BF16),
            pltpu.VMEM((wraps, order, columns), BF16),
            pltpu.VMEM((wraps, columns, order), BF16),
            pltpu.VMEM((wraps, columns, order), BF16),
            pltpu.VMEM((order, columns), F32),
            dma((3,)),
            dma((n_chunks,)),
            dma((n_chunks,)),
            dma((n_chunks,)),
            dma((n_chunks,)),
            dma((wraps,)),
            dma((wraps,)),
            dma((2, wraps)),
            dma((2, wraps)),
        ],
        compiler_params=pltpu.CompilerParams(
            collective_id=0, has_side_effects=True, vmem_limit_bytes=62 * 1024 * 1024
        ),
    )(seed_green, field_spins, hop_matrix, vertex)


def solution(mesh):
    body = functools.partial(per_device, mesh.shape["rowt"], mesh.shape["colt"])
    return jax.shard_map(
        body,
        mesh=mesh,
        in_specs=(
            P(("groups", "rowt"), "colt", None, "site"),
            P(None, ("groups", "rowt"), None),
            P(),
            P(),
        ),
        out_specs=P(("groups", "rowt"), "colt", None, "site"),
        check_vma=False,
    )
```

```python
import functools

import jax
import jax.numpy as jnp
from jax import lax
from jax.experimental import pallas as pl
from jax.experimental.pallas import tpu as pltpu
from jax.sharding import PartitionSpec as P

coupling = 0.45
keep_share = 0.8
hop_share = 0.3
MESH = pl.DeviceIdType.MESH
F32 = jnp.float32
BF16 = jnp.bfloat16


def split(x):
    high = x.astype(BF16)
    return high, (x - high.astype(F32)).astype(BF16)


def nn(a, b):
    return lax.dot_general(a, b, (((1,), (0,)), ((), ())), preferred_element_type=F32)


def nt(a, b):
    return lax.dot_general(a, b, (((1,), (1,)), ((), ())), preferred_element_type=F32)


def kernel(
    rows_n, cols_n,
    seed, spins, hop, vertex, out,
    own, hop_v, vertex_v, spin_v, theirs, a_hi, a_lo, x_hi, x_lo, y_hi, y_lo, m_hi, m_lo, total_v,
    local_sem, seed_send, seed_recv, pass_send, pass_recv, spin_send, spin_recv, cross_send,
    cross_recv,
):
    order, columns = own.shape
    wraps = spins.shape[0]
    row = lax.axis_index("rowt")
    col = lax.axis_index("colt")
    site = lax.axis_index("site")
    other_site = 1 - site
    other_col = lax.rem(col + cols_n // 2, cols_n)
    lanes = 128
    chunks = columns // lanes
    own_lanes = pl.ds(pl.multiple_of(site * columns, lanes), columns)
    row_of_other = pl.ds(pl.multiple_of(other_site * columns, lanes), columns)
    row_of_own = pl.ds(pl.multiple_of(site * columns, lanes), columns)

    local = [
        pltpu.make_async_copy(seed.at[0, 0], own, local_sem.at[0]),
        pltpu.make_async_copy(hop, hop_v, local_sem.at[1]),
        pltpu.make_async_copy(vertex, vertex_v, local_sem.at[2]),
    ]
    for copy in local:
        copy.start()

    distances = sorted({(w + 1) % rows_n for w in range(wraps)} - {0})
    peers = sorted(set(distances) | {(-d) % rows_n for d in distances})
    barrier = pltpu.get_barrier_semaphore()
    for peer in peers:
        pl.semaphore_signal(
            barrier, inc=1, device_id={"rowt": lax.rem(row + peer, rows_n)}, device_id_type=MESH
        )
    pl.semaphore_signal(barrier, inc=1, device_id={"colt": other_col}, device_id_type=MESH)
    pl.semaphore_signal(barrier, inc=1, device_id={"site": other_site}, device_id_type=MESH)
    pl.semaphore_wait(barrier, len(peers) + 2)

    spin_copies = []
    for w in range(wraps):
        distance = (w + 1) % rows_n
        if distance == 0:
            copy = pltpu.make_async_copy(spins.at[w], spin_v.at[w], spin_recv.at[w])
        else:
            copy = pltpu.make_async_remote_copy(
                src_ref=spins.at[w],
                dst_ref=spin_v.at[w],
                send_sem=spin_send.at[w],
                recv_sem=spin_recv.at[w],
                device_id={"rowt": lax.rem(row + rows_n - distance, rows_n)},
                device_id_type=MESH,
            )
        copy.start()
        spin_copies.append(copy)
    seed_copies, pass_copies = [], []
    for c in range(chunks):
        spot = pl.ds(pl.multiple_of(site * columns + c * lanes, lanes), lanes)
        seed_copies.append(pltpu.make_async_remote_copy(
            src_ref=seed.at[0, 0, :, pl.ds(c * lanes, lanes)],
            dst_ref=theirs.at[:, spot],
            send_sem=seed_send.at[c],
            recv_sem=seed_recv.at[c],
            device_id={"colt": other_col},
            device_id_type=MESH,
        ))
        pass_copies.append(pltpu.make_async_remote_copy(
            src_ref=theirs.at[:, spot],
            dst_ref=theirs.at[:, spot],
            send_sem=pass_send.at[c],
            recv_sem=pass_recv.at[c],
            device_id={"site": other_site},
            device_id_type=MESH,
        ))
        seed_copies[c].start()

    def pass_on(c):
        seed_copies[c].wait_recv()
        pass_copies[c].start()

    local[1].wait()
    step = 128
    for r in range(0, order, step):
        a = hop_share * hop_v[r:r + step, :]
        diagonal = lax.broadcasted_iota(jnp.int32, a.shape, 0) + r == lax.broadcasted_iota(
            jnp.int32, a.shape, 1
        )
        high, low = split(a + jnp.where(diagonal, F32(keep_share), F32(0)))
        a_hi[r:r + step, :] = high
        a_lo[r:r + step, :] = low

    local[0].wait()
    x0 = own[...].T

    def weight_row(w):
        sign = jnp.where(lax.rem(row + w + 1, rows_n) == 0, F32(-1), F32(1))
        return sign * jnp.exp(coupling * (2.0 * spin_v[w].astype(F32) - 1.0))

    tile = order
    cross_copies = []
    for w in range(wraps):
        products = []
        for n in range(0, order, tile):
            high = a_hi[n:n + tile, :]
            low = a_lo[n:n + tile, :]
            if w == 0:
                product = nt(x0, high) + nt(x0, low)
            else:
                before = x_hi[w - 1]
                product = nt(before, high) + nt(before, low) + nt(x_lo[(w - 1) % 2], high)
            if n == 0:
                spin_copies[w].wait()
                weights = weight_row(w)
            high, low = split(product * weights[:, n:n + tile])
            x_hi[w, :, n:n + tile] = high
            if w < wraps - 1:
                x_lo[w % 2, :, n:n + tile] = low
        if w == 0:
            product = a_hi[:, own_lanes].astype(F32) + a_lo[:, own_lanes].astype(F32)
        else:
            product = (
                nn(a_hi[...], y_hi[w - 1]) + nn(a_lo[...], y_hi[w - 1])
                + nn(a_hi[...], y_lo[w - 1])
            )
        column = jnp.broadcast_to(weights, (lanes, order)).T
        high, low = split(product * jnp.concatenate([column] * chunks, axis=1))
        for part, (value, held, whole) in enumerate(((high, y_hi, m_hi), (low, y_lo, m_lo))):
            held[w] = value
            copy = pltpu.make_async_remote_copy(
                src_ref=held.at[w, row_of_other],
                dst_ref=whole.at[w, :, own_lanes],
                send_sem=cross_send.at[part, w],
                recv_sem=cross_recv.at[part, w],
                device_id={"site": other_site},
                device_id_type=MESH,
            )
            copy.start()
            cross_copies.append(copy)
            whole[w, :, own_lanes] = held[w, row_of_own]
        if w == wraps - 2:
            pass_on(0)

    def both(c):
        return [s * columns + c * lanes for s in range(2)]

    def take(ref, index, c):
        return jnp.concatenate([ref[index + (slice(a, a + lanes),)] for a in both(c)], axis=1)

    def pair_sum(c):
        pass_copies[c].wait_recv()
        block = take(theirs, (slice(None),), c)
        total = None
        for w in range(wraps):
            far = (nn(m_hi[w], block) + nn(m_lo[w], block)).astype(BF16)
            near = take(x_hi, (w, slice(None)), c)
            pair = (near.astype(F32) * far.astype(F32)).astype(BF16).astype(F32)
            total = pair if total is None else total + pair
        return split(total)

    if wraps < 2:
        pass_on(0)
    if chunks > 2:
        pass_on(1)
    for copy in cross_copies:
        copy.wait_recv()
    sums = []
    for c in range(chunks - 1):
        if 1 < c + 1 < chunks - 1:
            pass_on(c + 1)
        sums.append(pair_sum(c))
    if chunks > 1:
        pass_on(chunks - 1)
    local[2].wait()
    high = jnp.concatenate([h for h, _ in sums], axis=1)
    low = jnp.concatenate([l for _, l in sums], axis=1)
    for m in range(0, order, tile):
        rows = slice(m, m + tile)
        v = jnp.concatenate([take(vertex_v, (rows,), c) for c in range(chunks - 1)], axis=1)
        total_v[rows] = nt(v, high) + nt(v, low)
    high, low = pair_sum(chunks - 1)
    for m in range(0, order, tile):
        rows = slice(m, m + tile)
        v = take(vertex_v, (rows,), chunks - 1)
        total = total_v[rows] + nt(v, high) + nt(v, low)
        out[0, 0, rows] = (total / wraps).astype(BF16)

    for copy in seed_copies + pass_copies + cross_copies:
        copy.wait_send()


def per_device(rows_n, cols_n, seed_green, field_spins, hop_matrix, vertex):
    wraps = field_spins.shape[0]
    order, columns = seed_green.shape[2:]
    n_chunks = columns // 128
    dma = pltpu.SemaphoreType.DMA
    any_space = pl.BlockSpec(memory_space=pl.ANY)
    return pl.pallas_call(
        functools.partial(kernel, rows_n, cols_n),
        out_shape=jax.ShapeDtypeStruct(seed_green.shape, BF16),
        in_specs=[any_space] * 4,
        out_specs=pl.BlockSpec(memory_space=pltpu.VMEM),
        scratch_shapes=[
            pltpu.VMEM((order, columns), BF16),
            pltpu.VMEM((order, order), F32),
            pltpu.VMEM((order, order), BF16),
            pltpu.VMEM((wraps, 1, order), jnp.int32),
            pltpu.VMEM((order, order), BF16),
            pltpu.VMEM((order, order), BF16),
            pltpu.VMEM((order, order), BF16),
            pltpu.VMEM((wraps, columns, order), BF16),
            pltpu.VMEM((2, columns, order), BF16),
            pltpu.VMEM((wraps, order, columns), BF16),
            pltpu.VMEM((wraps, order, columns), BF16),
            pltpu.VMEM((wraps, columns, order), BF16),
            pltpu.VMEM((wraps, columns, order), BF16),
            pltpu.VMEM((order, columns), F32),
            dma((3,)),
            dma((n_chunks,)),
            dma((n_chunks,)),
            dma((n_chunks,)),
            dma((n_chunks,)),
            dma((wraps,)),
            dma((wraps,)),
            dma((2, wraps)),
            dma((2, wraps)),
        ],
        compiler_params=pltpu.CompilerParams(
            collective_id=0, has_side_effects=True, vmem_limit_bytes=62 * 1024 * 1024
        ),
    )(seed_green, field_spins, hop_matrix, vertex)


def solution(mesh):
    body = functools.partial(per_device, mesh.shape["rowt"], mesh.shape["colt"])
    return jax.shard_map(
        body,
        mesh=mesh,
        in_specs=(
            P(("groups", "rowt"), "colt", None, "site"),
            P(None, ("groups", "rowt"), None),
            P(),
            P(),
        ),
        out_specs=P(("groups", "rowt"), "colt", None, "site"),
        check_vma=False,
    )
```
